256 devices in a mesh: vid: 64 (over y, z_hi, x), aud: 4 (over z_lo, core).
Axes of the slice: x: 4, y: 4, z: 8 (z_hi: 4, z_lo: 2; z = z_hi * 2 + z_lo), core: 2. Of those that a mesh axis runs over, the one named last changes fastest.
Arguments:
- video_query: bfloat16 [16384, 3072], P(('vid', 'aud')), may hold values from -66 to 66
- video_key: bfloat16 [16384, 3072], P(('vid', 'aud')), may hold values from -4 to 4
- video_value: bfloat16 [16384, 3072], P(('vid', 'aud')), may hold values from -6 to 6
- video_cotan: bfloat16 [16384, 3072], P(('vid', 'aud')), may hold values from -6 to 6
- audio_query: bfloat16 [1024, 3072], P('vid', 'aud'), may hold values from -66 to 66
- audio_key: bfloat16 [1024, 3072], P('vid', 'aud'), may hold values from -4 to 4
- audio_value: bfloat16 [1024, 3072], P('vid', 'aud'), may hold values from -6 to 6
- audio_cotan: bfloat16 [1024, 3072], P('vid', 'aud'), may hold values from -6 to 6
- alignment: int32 [1024], replicated, may hold values from 0 to 15, as said below
Outputs:
- video_cross_output: bfloat16 [16384, 3072], P(('vid', 'aud'))
- audio_cross_output: bfloat16 [1024, 3072], P('vid', 'aud')
- video_query_grad: bfloat16 [16384, 3072], P(('vid', 'aud'))
- video_key_grad: bfloat16 [16384, 3072], P(('vid', 'aud'))
- video_value_grad: bfloat16 [16384, 3072], P(('vid', 'aud'))
- audio_query_grad: bfloat16 [1024, 3072], P('vid', 'aud')
- audio_key_grad: bfloat16 [1024, 3072], P('vid', 'aud')
- audio_value_grad: bfloat16 [1024, 3072], P('vid', 'aud')
The draws below stay inside these ranges and needn't reach their ends.
Inputs may be any that keep to these rules, and one draw needn't show every extreme that they name: `alignment`: non-decreasing along the audio tokens; the first is 0 and the last 15.
All inputs are finite; a program needn't handle non-finite values.
Results may differ from the reference program's by a relative error of at most 0.035.
Values may be sent and summed in bfloat16 or wider, within the bound.
No kernel may reach another device: no remote copies, remote signals or barrier semaphores. Data moves between devices by JAX's collectives and lax.ppermute only.
A program may use at most 128 MiB of HBM per device.

```python
import jax
import jax.numpy as jnp
from jax import lax

H = 24
DH = 128
FRAMES = 16
VTOK = 16384
ATOK = 1024


def draw_video_query(key, part):
    key = jax.random.fold_in(key, 1)
    field = jnp.clip(jax.random.normal(key, (VTOK, H * DH), jnp.float32), -4.0, 4.0)
    return field.astype(jnp.bfloat16)


def draw_audio_key(key, part):
    key = jax.random.fold_in(key, 2)
    field = jnp.clip(jax.random.normal(key, (ATOK, H * DH), jnp.float32), -4.0, 4.0)
    return field.astype(jnp.bfloat16)


def draw_audio_query(key, part):
    key = jax.random.fold_in(key, 3)
    field = jnp.clip(jax.random.normal(key, (ATOK, H * DH), jnp.float32), -4.0, 4.0)
    return field.astype(jnp.bfloat16)


def draw_video_key(key, part):
    key = jax.random.fold_in(key, 4)
    field = jnp.clip(jax.random.normal(key, (VTOK, H * DH), jnp.float32), -4.0, 4.0)
    return field.astype(jnp.bfloat16)


def draw_alignment(key, part):
    key = jax.random.fold_in(key, 5)
    steps = jnp.arange(ATOK, dtype=jnp.int32)
    base = steps * FRAMES // ATOK
    jitter = jax.random.randint(key, (ATOK,), -1, 2, dtype=jnp.int32)
    frames = jnp.clip(base + jitter, 0, FRAMES - 1)
    frames = jnp.sort(frames)
    frames = frames.at[0].set(0).at[ATOK - 1].set(FRAMES - 1)
    return frames.astype(jnp.int32)


def shard_levels(stream_key, dims, cuts, least, top_value):
    loudness = 1.0
    for position, shards_of in cuts:
        heights = jax.random.uniform(jax.random.fold_in(jax.random.fold_in(stream_key, 6), position), (shards_of,), jnp.float32, least / len(cuts), top_value / len(cuts))
        loudness = loudness * jnp.repeat(jnp.exp(heights), dims[position] // shards_of).reshape((-1,) + (1,) * (len(dims) - 1 - position))
    return loudness


def gaussian(key, extent, scale, limit, shards=(), kind=jnp.bfloat16):
    entries = jax.random.normal(key, extent, jnp.float32) * scale
    if len(shards) > 0:
        entries = shard_levels(key, extent, shards, -0.22, 0.18) * entries
    return jnp.clip(entries, min=-limit, max=limit).astype(kind)


def setup_inputs(seed: int = 0) -> dict:
    arg_keys = jax.random.split(jax.random.key(seed), 10)
    video_query = draw_video_query(jax.random.fold_in(arg_keys[9], 71), 0)
    video_key = draw_video_key(jax.random.fold_in(arg_keys[9], 71), 0)
    video_value = gaussian(arg_keys[2], (VTOK, H * DH), 1.0, 6.0, ((0, 256),))
    video_cotan = gaussian(arg_keys[3], (VTOK, H * DH), 1.0, 6.0, ((0, 256),))
    audio_query = draw_audio_query(jax.random.fold_in(arg_keys[9], 71), 0)
    audio_key = draw_audio_key(jax.random.fold_in(arg_keys[9], 71), 0)
    audio_value = gaussian(arg_keys[6], (ATOK, H * DH), 1.0, 6.0, ((0, 64), (1, 4)))
    audio_cotan = gaussian(arg_keys[7], (ATOK, H * DH), 1.0, 6.0, ((0, 64), (1, 4)))
    alignment = draw_alignment(jax.random.fold_in(arg_keys[9], 71), 0)
    return dict(video_query=video_query, video_key=video_key, video_value=video_value, video_cotan=video_cotan, audio_query=audio_query, audio_key=audio_key, audio_value=audio_value, audio_cotan=audio_cotan, alignment=alignment)


BIAS_SLOPE = 0.25


def cross_attend(queries, keys_in, values_in, cotangent, score_bias):
    score_scale = DH ** -0.5
    scores = jnp.dot(queries, keys_in.T, preferred_element_type=jnp.float32) * score_scale + score_bias
    peaks = jnp.max(scores, axis=1, keepdims=True)
    raised = jnp.exp(scores - peaks)
    totals = jnp.sum(raised, axis=1, keepdims=True)
    output = jnp.dot(raised.astype(jnp.bfloat16), values_in, preferred_element_type=jnp.float32) / totals
    probs = raised / totals
    inner = jnp.sum(cotangent.astype(jnp.float32) * output, axis=1, keepdims=True)
    dprobs = jnp.dot(cotangent, values_in.T, preferred_element_type=jnp.float32)
    dscores = (probs * (dprobs - inner)).astype(jnp.bfloat16)
    query_grad = jnp.dot(dscores, keys_in, preferred_element_type=jnp.float32) * score_scale
    key_grad = jnp.dot(dscores.T, queries, preferred_element_type=jnp.float32) * score_scale
    value_grad = jnp.dot(probs.astype(jnp.bfloat16).T, cotangent, preferred_element_type=jnp.float32)
    return output, query_grad, key_grad, value_grad


def split_into_heads(array):
    return jnp.transpose(array.reshape(array.shape[0], H, DH), (1, 0, 2))


def heads_to_rows(array):
    return jnp.transpose(array, (1, 0, 2)).reshape(array.shape[1], H * DH).astype(jnp.bfloat16)


def reference(video_query, video_key, video_value, video_cotan, audio_query, audio_key, audio_value, audio_cotan, alignment):
    frame_tok = VTOK // FRAMES
    frames = (jnp.arange(VTOK, dtype=jnp.int32) // frame_tok).astype(jnp.int32)
    score_bias = -BIAS_SLOPE * jnp.abs(frames[:, None] - alignment[None, :].astype(jnp.int32)).astype(jnp.float32)

    def one_head(output_portions):
        video_query_rows, video_key_rows, video_value_rows, video_output_cotangent, audio_query_rows, audio_key_rows, audio_value_rows, audio_output_cotangent = output_portions
        video_part = cross_attend(video_query_rows, audio_key_rows, audio_value_rows, video_output_cotangent, score_bias)
        audio_portion = cross_attend(audio_query_rows, video_key_rows, video_value_rows, audio_output_cotangent, score_bias.T)
        return video_part + audio_portion

    stacked = (split_into_heads(video_query), split_into_heads(video_key), split_into_heads(video_value), split_into_heads(video_cotan),
               split_into_heads(audio_query), split_into_heads(audio_key), split_into_heads(audio_value), split_into_heads(audio_cotan))
    gradient_results = lax.map(one_head, stacked)
    video_cross_output, video_query_gradient, audio_key_gradient, audio_value_gradient, audio_cross_output, audio_query_gradient, video_key_gradient, video_value_gradient = gradient_results
    return (heads_to_rows(video_cross_output), heads_to_rows(audio_cross_output), heads_to_rows(video_query_gradient), heads_to_rows(video_key_gradient),
            heads_to_rows(video_value_gradient), heads_to_rows(audio_query_gradient), heads_to_rows(audio_key_gradient), heads_to_rows(audio_value_gradient))
```

```python
import math

import jax
import jax.numpy as jnp
from jax import lax
from jax.experimental import pallas as pl
from jax.experimental.pallas import tpu as pltpu
from jax.sharding import Mesh
from jax.sharding import PartitionSpec as P

DH = 128
FRAMES = 16
BIAS_SLOPE = 0.25
SCALE = DH ** (-0.5)
LOG2E = math.log2(math.e)

AXES = (("y", 4), ("zh", 4), ("xh", 2), ("xl", 2), ("zl", 2), ("core", 2))
NAMES = tuple(name for name, _ in AXES)
VID = ("y", "zh", "xh", "xl")
AUD = ("zl", "core")
HEADS8 = ("zl", "core", "xl")
PLANE = ("zh", "xh", "xl")
VMEM = 56 * 1024 * 1024
LONG = pl.CostEstimate(flops=5 * 10 ** 10, bytes_accessed=0, transcendentals=0)


def mm(a, b, contract):
    return lax.dot_general(
        a, b, ((contract[0], contract[1]), ((), ())), preferred_element_type=jnp.float32
    )


def rows_of(ref, array):
    return ref[:, array].reshape(ref.shape[0] * ref.shape[2], DH)


def audio_stats_kernel(start, qg0, qg1, qg2, qg3, kv, out):
    rows = kv.shape[0] * kv.shape[2]
    keys, values = rows_of(kv, 0), rows_of(kv, 1)
    for block, ref in enumerate((qg0, qg1, qg2, qg3)):
        width = ref.shape[0] * ref.shape[2]
        lanes = pl.ds(pl.multiple_of(start[block], width), width)
        scores = mm(keys, rows_of(ref, 0), ((1,), (1,)))
        peak = jnp.max(scores, axis=0, keepdims=True)
        raised = jnp.exp2((scores - peak) * (SCALE * LOG2E))
        total = jnp.sum(raised, axis=0, keepdims=True)
        dprobs = mm(values, rows_of(ref, 1), ((1,), (1,)))
        inner = jnp.sum(raised * dprobs, axis=0, keepdims=True)
        out[0, 0:1, lanes] = peak * SCALE + jnp.log(total)
        out[0, 1:2, lanes] = inner / total


def audio_grad_kernel(
    start, qg0, qg1, qg2, qg3, kv, stats, od0, od1, od2, od3, *refs
):
    kvgrad, probs_all, ds_all = refs[:8], refs[8], refs[9]
    keys = jnp.concatenate([kv[start[4 + m], 0] for m in range(8)], axis=0)
    values = jnp.concatenate([kv[start[4 + m], 1] for m in range(8)], axis=0)
    queries, cotans = [], []
    for block, (ref, dst) in enumerate(zip((qg0, qg1, qg2, qg3), (od0, od1, od2, od3))):
        width = ref.shape[0] * ref.shape[2]
        lanes = pl.ds(pl.multiple_of(start[block], width), width)
        query = rows_of(ref, 0)
        cotan = rows_of(ref, 1)
        queries.append(query)
        cotans.append(cotan)
        scores = mm(keys, query, ((1,), (1,)))
        probs = jnp.exp2(scores * (SCALE * LOG2E) - stats[0, 0:1, lanes] * LOG2E)
        dprobs = mm(values, cotan, ((1,), (1,)))
        dscores = (probs * (dprobs - stats[0, 1:2, lanes])).astype(jnp.bfloat16)
        probs = probs.astype(jnp.bfloat16)
        here = slice(block * width, (block + 1) * width)
        probs_all[:, here] = probs
        ds_all[:, here] = dscores
        out = jnp.transpose(mm(values, probs, ((0,), (0,)))).astype(jnp.bfloat16)
        qgrad = jnp.transpose(mm(keys, dscores, ((0,), (0,))) * SCALE).astype(jnp.bfloat16)
        shape = (ref.shape[0], ref.shape[2], DH)
        dst[:, 0] = out.reshape(shape)
        dst[:, 1] = qgrad.reshape(shape)
    kgrad = mm(ds_all[...], jnp.concatenate(queries, axis=0), ((1,), (0,))) * SCALE
    vgrad = mm(probs_all[...], jnp.concatenate(cotans, axis=0), ((1,), (0,)))
    for m, dst in enumerate(kvgrad):
        group = dst.shape[1]
        dst[0] = kgrad[m * group:(m + 1) * group].astype(jnp.bfloat16)
        dst[1] = vgrad[m * group:(m + 1) * group].astype(jnp.bfloat16)


def unpack_kernel(start, *refs):
    first, second = refs[8:]
    for m, ref in enumerate(refs[:8]):
        width = ref.shape[2]
        columns = pl.ds(pl.multiple_of(start[4 + m] * width, DH), width)
        first[:, columns] = ref[0]
        second[:, columns] = ref[1]


def video_kernel(kv0, kv1, kv2, kv3, qg, bias, kvg0, kvg1, kvg2, kvg3, oqgrad, probs_all, ds_all):
    width = kv0.shape[0] * kv0.shape[2]
    group = qg.shape[2]
    rows = qg.shape[0] * group
    query_all, cotan_all = rows_of(qg, 0), rows_of(qg, 1)
    refs = (kv0, kv1, kv2, kv3)
    keys = jnp.concatenate([rows_of(ref, 0) for ref in refs], axis=0)
    values = jnp.concatenate([rows_of(ref, 1) for ref in refs], axis=0)
    chunk = 256
    for start in range(0, rows, chunk):
        query = query_all[start:start + chunk]
        cotan = cotan_all[start:start + chunk]
        shift = jnp.concatenate([bias[...]] * (chunk // DH), axis=1)
        scores = mm(keys, query, ((1,), (1,))) * (SCALE * LOG2E) + shift
        peak = jnp.max(scores, axis=0, keepdims=True)
        raised = jnp.exp2(scores - peak)
        total = jnp.sum(raised, axis=0, keepdims=True)
        probs = raised * (1.0 / total)
        dprobs = mm(values, cotan, ((1,), (1,)))
        inner = jnp.sum(probs * dprobs, axis=0, keepdims=True)
        dscores = (probs * (dprobs - inner)).astype(jnp.bfloat16)
        probs = probs.astype(jnp.bfloat16)
        probs_all[:, start:start + chunk] = probs
        ds_all[:, start:start + chunk] = dscores
        out = mm(values, probs, ((0,), (0,)))
        qgrad = mm(keys, dscores, ((0,), (0,))) * SCALE
        at = pl.ds(start // group, chunk // group)
        shape = (chunk // group, group, DH)
        oqgrad[at, 0] = jnp.transpose(out).astype(jnp.bfloat16).reshape(shape)
        oqgrad[at, 1] = jnp.transpose(qgrad).astype(jnp.bfloat16).reshape(shape)
    kgrad = (mm(ds_all[...], query_all, ((1,), (0,))) * SCALE).astype(jnp.bfloat16)
    vgrad = mm(probs_all[...], cotan_all, ((1,), (0,))).astype(jnp.bfloat16)
    for block, dst in enumerate((kvg0, kvg1, kvg2, kvg3)):
        shape = (dst.shape[0], dst.shape[2], DH)
        dst[:, 0] = kgrad[block * width:(block + 1) * width].reshape(shape)
        dst[:, 1] = vgrad[block * width:(block + 1) * width].reshape(shape)


def head_block(shape, pair=0):
    block = (shape[0], 2) + tuple(shape[2:-1]) + (DH,)
    return pl.BlockSpec(block, lambda h: (0, pair, 0, h))


def sizes(blocks, video):
    tokens = len(blocks) * blocks[0].shape[0] * blocks[0].shape[2]
    return video.shape[0] * video.shape[2], tokens, video.shape[-1] // DH


def audio_stats(start, blocks, video):
    rows, tokens, heads = sizes(blocks, video)
    return pl.pallas_call(
        audio_stats_kernel,
        grid=(heads,),
        in_specs=[pl.BlockSpec(memory_space=pltpu.SMEM)]
        + [head_block(b.shape) for b in blocks]
        + [head_block(video.shape)],
        out_specs=pl.BlockSpec((1, 2, tokens), lambda h: (h, 0, 0)),
        out_shape=jax.ShapeDtypeStruct((heads, 2, tokens), jnp.float32),
        compiler_params=pltpu.CompilerParams(vmem_limit_bytes=VMEM),
        cost_estimate=LONG,
        name="audio_stats",
    )(start, *blocks, video)


def audio_grad(start, blocks, video, stats):
    rows, tokens, heads = sizes(blocks, video)
    part = jax.ShapeDtypeStruct((2,) + video.shape[2:], jnp.bfloat16)
    part_block = pl.BlockSpec(part.shape[:2] + (DH,), lambda h: (0, 0, h))
    block = jax.ShapeDtypeStruct(blocks[0].shape, jnp.bfloat16)
    result = pl.pallas_call(
        audio_grad_kernel,
        grid=(heads,),
        in_specs=[pl.BlockSpec(memory_space=pltpu.SMEM)]
        + [head_block(b.shape) for b in blocks]
        + [head_block(video.shape), pl.BlockSpec((1, 2, tokens), lambda h: (h, 0, 0))],
        out_specs=[head_block(b.shape) for b in blocks] + [part_block] * 8,
        out_shape=[block] * 4 + [part] * 8,
        scratch_shapes=[pltpu.VMEM((rows, tokens), jnp.bfloat16)] * 2,
        compiler_params=pltpu.CompilerParams(vmem_limit_bytes=VMEM),
        cost_estimate=LONG,
        name="audio_grad",
    )(start, *blocks, video, stats)
    return result[:4], result[4:]


def unpack(start, parts):
    _, rows, columns = parts[0].shape
    out = jax.ShapeDtypeStruct((rows, columns * 8), parts[0].dtype)
    in_vmem = pl.BlockSpec(memory_space=pltpu.VMEM)
    return pl.pallas_call(
        unpack_kernel,
        in_specs=[pl.BlockSpec(memory_space=pltpu.SMEM)] + [in_vmem] * 8,
        out_specs=[in_vmem] * 2,
        out_shape=[out] * 2,
        name="unpack",
    )(start, *parts)


def swap(parts):
    axes = ("xl", "zl", "core")
    masks = [(m & 1) * 4 + m // 2 for m in range(8)]
    return [parts[0]] + [
        lax.ppermute(parts[m], axes, [(i, i ^ masks[m]) for i in range(8)]) for m in range(1, 8)
    ]


def video_all(blocks, video, bias):
    rows, tokens, heads = sizes(blocks, video)
    pair = jax.ShapeDtypeStruct((video.shape[0], 2) + video.shape[2:], jnp.bfloat16)
    block = jax.ShapeDtypeStruct(blocks[0].shape, jnp.bfloat16)
    result = pl.pallas_call(
        video_kernel,
        grid=(heads,),
        in_specs=[head_block(b.shape) for b in blocks]
        + [head_block(video.shape, 1), pl.BlockSpec((tokens, DH), lambda h: (0, 0))],
        out_specs=[head_block(b.shape) for b in blocks] + [head_block(video.shape)],
        out_shape=[block] * 4 + [pair],
        scratch_shapes=[pltpu.VMEM((tokens, rows), jnp.bfloat16)] * 2,
        compiler_params=pltpu.CompilerParams(vmem_limit_bytes=VMEM),
        cost_estimate=LONG,
        name="video_all",
    )(*blocks, video, bias)
    return result[:4], result[4]


def exchange(x, axes):
    return lax.all_to_all(x, axes, split_axis=0, concat_axis=0)


def after(x, *others):
    return lax.optimization_barrier((x,) + others)[0]


def video_in(arrays, *others):
    rows, columns = arrays[0].shape
    stack = jnp.stack(arrays).reshape(len(arrays), rows, 8, columns // 8)
    return exchange(after(jnp.transpose(stack, (2, 0, 1, 3)), *others), HEADS8)


def video_out(pair, *others):
    back = jnp.transpose(exchange(after(pair, *others), HEADS8), (1, 2, 0, 3))
    back = back.reshape(2, back.shape[1], -1)
    return back[0], back[1]


def plane_in(arrays):
    stack = jnp.stack(arrays)
    half = stack.shape[-1] // 2
    halves = jnp.stack([stack[..., :half], stack[..., half:]])
    sends = jnp.broadcast_to(halves[None], (8,) + halves.shape)
    return exchange(sends.reshape((16,) + halves.shape[1:]), PLANE)


def plane_out(x, *others):
    got = exchange(after(x, *others), PLANE)
    got = got.reshape((8, 2) + got.shape[1:]).astype(jnp.float32).sum(axis=0)
    return jnp.concatenate([got[0], got[1]], axis=-1).astype(jnp.bfloat16)


def along_y(x, step):
    return lax.ppermute(x, "y", [(i, (i + step) % 4) for i in range(4)])


def gather_y(x):
    return [x] + [along_y(x, -step) for step in (1, 2, 3)]


def scatter_y(blocks):
    return [blocks[0]] + [along_y(blocks[step], step) for step in (1, 2, 3)]


def add(parts):
    return sum(part.astype(jnp.float32) for part in parts).astype(jnp.bfloat16)


def merge_stats(stats, axis):
    levels, means = stats
    top = jnp.max(levels, axis=axis, keepdims=True)
    weights = jnp.exp(levels - top)
    total = jnp.sum(weights, axis=axis, keepdims=True)
    mean = jnp.sum(weights * means, axis=axis, keepdims=True) / total
    return jnp.squeeze(top + jnp.log(total), axis), jnp.squeeze(mean, axis)


def per_device(
    video_query,
    video_key,
    video_value,
    video_cotan,
    audio_query,
    audio_key,
    audio_value,
    audio_cotan,
    alignment,
):
    y, zh = lax.axis_index("y"), lax.axis_index("zh")
    frame = y * 4 + zh
    tokens = alignment.shape[0]
    bias = -BIAS_SLOPE * jnp.abs(frame - alignment).astype(jnp.float32)
    start = ((y + jnp.arange(4, dtype=jnp.int32)) % 4) * (tokens // 4)
    place = lax.axis_index("zl") * 4 + lax.axis_index("core") * 2 + lax.axis_index("xl")
    start = jnp.concatenate([start, place ^ jnp.arange(8, dtype=jnp.int32)]).astype(jnp.int32)
    turned = lax.dynamic_slice_in_dim(jnp.tile(bias, 2), start[0], tokens)
    key_bias = jnp.broadcast_to((turned * LOG2E)[:, None], (tokens, DH))

    planes = plane_in([audio_query, audio_cotan, audio_key, audio_value])
    video = video_in([video_key, video_value, video_query, video_cotan], planes)
    audio_qg = gather_y(planes[:, :2])
    audio_kv = gather_y(after(planes[:, 2:], audio_qg[1], audio_qg[3]))

    stats = audio_stats(start, audio_qg, video)
    stats = after(jnp.stack([stats[:, 0] + bias, stats[:, 1]]), audio_kv[1], audio_kv[3])
    seen = jnp.stack(merge_stats(jnp.stack(gather_y(stats), axis=1), 0))
    key_bias = after(key_bias, seen)
    seen = exchange(jnp.broadcast_to(seen[None], (8,) + seen.shape), ("zh", "xh"))
    level, inner = merge_stats((seen[:, 0], seen[:, 1]), 0)
    stats = jnp.stack([level - bias, inner], axis=1)

    key_value_blocks, video_oq = video_all(audio_kv, video, key_bias)
    out_query_blocks, video_kvgrad = audio_grad(start, audio_qg, video, stats)

    parts = scatter_y(key_value_blocks)
    video_cross_output, video_query_grad = video_out(video_oq)
    gate = (video_query_grad,) + tuple(parts[1:])
    video_kvgrad = lax.optimization_barrier(tuple(video_kvgrad) + gate)[:8]
    video_kvgrad = swap(video_kvgrad)
    video_key_grad, video_value_grad = unpack(start, video_kvgrad)
    sums = plane_out(add(parts), video_query_grad, out_query_blocks[0])
    audio_key_grad, audio_value_grad = sums
    parts = scatter_y(out_query_blocks)
    parts = lax.optimization_barrier(tuple(parts) + tuple(video_kvgrad))[:4]
    sums = plane_out(add(parts), audio_key_grad)
    audio_cross_output, audio_query_grad = sums
    return (
        video_cross_output,
        audio_cross_output,
        video_query_grad,
        video_key_grad,
        video_value_grad,
        audio_query_grad,
        audio_key_grad,
        audio_value_grad,
    )


def solution(mesh):
    split = Mesh(mesh.devices.reshape(tuple(size for _, size in AXES)), NAMES)
    video = P(NAMES, None)
    audio = P(VID, AUD)
    return jax.shard_map(
        per_device,
        mesh=split,
        in_specs=(video,) * 4 + (audio,) * 4 + (P(),),
        out_specs=(video, audio, video, video, video, audio, audio, audio),
        check_vma=False,
    )
```

```python
import math

import jax
import jax.numpy as jnp
from jax import lax
from jax.experimental import pallas as pl
from jax.experimental.pallas import tpu as pltpu
from jax.sharding import Mesh
from jax.sharding import PartitionSpec as P

DH = 128
FRAMES = 16
BIAS_SLOPE = 0.25
SCALE = DH ** (-0.5)
LOG2E = math.log2(math.e)

AXES = (("y", 4), ("zh", 4), ("xh", 2), ("xl", 2), ("zl", 2), ("core", 2))
NAMES = tuple(name for name, _ in AXES)
VID = ("y", "zh", "xh", "xl")
AUD = ("zl", "core")
HEADS8 = ("zl", "core", "xl")
PLANE = ("zh", "xh", "xl")
VMEM = 56 * 1024 * 1024
LONG = pl.CostEstimate(flops=5 * 10 ** 10, bytes_accessed=0, transcendentals=0)


def mm(a, b, contract):
    return lax.dot_general(
        a, b, ((contract[0], contract[1]), ((), ())), preferred_element_type=jnp.float32
    )


def rows_of(ref, array):
    return ref[:, array].reshape(ref.shape[0] * ref.shape[2], DH)


def audio_stats_kernel(start, qg0, qg1, qg2, qg3, kv, out):
    rows = kv.shape[0] * kv.shape[2]
    keys, values = rows_of(kv, 0), rows_of(kv, 1)
    for block, ref in enumerate((qg0, qg1, qg2, qg3)):
        width = ref.shape[0] * ref.shape[2]
        lanes = pl.ds(pl.multiple_of(start[block], width), width)
        scores = mm(keys, rows_of(ref, 0), ((1,), (1,)))
        peak = jnp.max(scores, axis=0, keepdims=True)
        raised = jnp.exp2((scores - peak) * (SCALE * LOG2E))
        total = jnp.sum(raised, axis=0, keepdims=True)
        dprobs = mm(values, rows_of(ref, 1), ((1,), (1,)))
        inner = jnp.sum(raised * dprobs, axis=0, keepdims=True)
        out[0, 0:1, lanes] = peak * SCALE + jnp.log(total)
        out[0, 1:2, lanes] = inner / total


def audio_grad_kernel(
    start, qg0, qg1, qg2, qg3, kv, stats, video_grads, od0, od1, od2, od3, kvgrad, probs_all, ds_all
):
    rows = kv.shape[0] * kv.shape[2]
    keys, values = rows_of(kv, 0), rows_of(kv, 1)
    queries, cotans = [], []
    for block, (ref, dst) in enumerate(zip((qg0, qg1, qg2, qg3), (od0, od1, od2, od3))):
        width = ref.shape[0] * ref.shape[2]
        lanes = pl.ds(pl.multiple_of(start[block], width), width)
        query = rows_of(ref, 0)
        cotan = rows_of(ref, 1)
        queries.append(query)
        cotans.append(cotan)
        scores = mm(keys, query, ((1,), (1,)))
        probs = jnp.exp2(scores * (SCALE * LOG2E) - stats[0, 0:1, lanes] * LOG2E)
        dprobs = mm(values, cotan, ((1,), (1,)))
        dscores = (probs * (dprobs - stats[0, 1:2, lanes])).astype(jnp.bfloat16)
        probs = probs.astype(jnp.bfloat16)
        here = slice(block * width, (block + 1) * width)
        probs_all[:, here] = probs
        ds_all[:, here] = dscores
        out = jnp.transpose(mm(values, probs, ((0,), (0,)))).astype(jnp.bfloat16)
        qgrad = jnp.transpose(mm(keys, dscores, ((0,), (0,))) * SCALE).astype(jnp.bfloat16)
        shape = (ref.shape[0], ref.shape[2], DH)
        dst[:, 0] = out.reshape(shape)
        dst[:, 1] = qgrad.reshape(shape)
    shape = (kv.shape[0], kv.shape[2], DH)
    kgrad = mm(ds_all[...], jnp.concatenate(queries, axis=0), ((1,), (0,))) * SCALE
    kvgrad[:, 0] = kgrad.astype(jnp.bfloat16).reshape(shape)
    vgrad = mm(probs_all[...], jnp.concatenate(cotans, axis=0), ((1,), (0,)))
    kvgrad[:, 1] = vgrad.astype(jnp.bfloat16).reshape(shape)


def video_kernel(kv0, kv1, kv2, kv3, qg, bias, kvg0, kvg1, kvg2, kvg3, oqgrad, probs_all, ds_all):
    width = kv0.shape[0] * kv0.shape[2]
    group = qg.shape[2]
    rows = qg.shape[0] * group
    query_all, cotan_all = rows_of(qg, 0), rows_of(qg, 1)
    refs = (kv0, kv1, kv2, kv3)
    keys = jnp.concatenate([rows_of(ref, 0) for ref in refs], axis=0)
    values = jnp.concatenate([rows_of(ref, 1) for ref in refs], axis=0)
    chunk = 256
    for start in range(0, rows, chunk):
        query = query_all[start:start + chunk]
        cotan = cotan_all[start:start + chunk]
        shift = jnp.concatenate([bias[...]] * (chunk // DH), axis=1)
        scores = mm(keys, query, ((1,), (1,))) * (SCALE * LOG2E) + shift
        peak = jnp.max(scores, axis=0, keepdims=True)
        raised = jnp.exp2(scores - peak)
        total = jnp.sum(raised, axis=0, keepdims=True)
        probs = raised * (1.0 / total)
        dprobs = mm(values, cotan, ((1,), (1,)))
        inner = jnp.sum(probs * dprobs, axis=0, keepdims=True)
        dscores = (probs * (dprobs - inner)).astype(jnp.bfloat16)
        probs = probs.astype(jnp.bfloat16)
        probs_all[:, start:start + chunk] = probs
        ds_all[:, start:start + chunk] = dscores
        out = mm(values, probs, ((0,), (0,)))
        qgrad = mm(keys, dscores, ((0,), (0,))) * SCALE
        at = pl.ds(start // group, chunk // group)
        shape = (chunk // group, group, DH)
        oqgrad[at, 0] = jnp.transpose(out).astype(jnp.bfloat16).reshape(shape)
        oqgrad[at, 1] = jnp.transpose(qgrad).astype(jnp.bfloat16).reshape(shape)
    kgrad = (mm(ds_all[...], query_all, ((1,), (0,))) * SCALE).astype(jnp.bfloat16)
    vgrad = mm(probs_all[...], cotan_all, ((1,), (0,))).astype(jnp.bfloat16)
    for block, dst in enumerate((kvg0, kvg1, kvg2, kvg3)):
        shape = (dst.shape[0], dst.shape[2], DH)
        dst[:, 0] = kgrad[block * width:(block + 1) * width].reshape(shape)
        dst[:, 1] = vgrad[block * width:(block + 1) * width].reshape(shape)


def head_block(shape, pair=0):
    block = (shape[0], 2) + tuple(shape[2:-1]) + (DH,)
    return pl.BlockSpec(block, lambda h: (0, pair, 0, h))


def sizes(blocks, video):
    tokens = len(blocks) * blocks[0].shape[0] * blocks[0].shape[2]
    return video.shape[0] * video.shape[2], tokens, video.shape[-1] // DH


def audio_stats(start, blocks, video):
    rows, tokens, heads = sizes(blocks, video)
    return pl.pallas_call(
        audio_stats_kernel,
        grid=(heads,),
        in_specs=[pl.BlockSpec(memory_space=pltpu.SMEM)]
        + [head_block(b.shape) for b in blocks]
        + [head_block(video.shape)],
        out_specs=pl.BlockSpec((1, 2, tokens), lambda h: (h, 0, 0)),
        out_shape=jax.ShapeDtypeStruct((heads, 2, tokens), jnp.float32),
        compiler_params=pltpu.CompilerParams(vmem_limit_bytes=VMEM),
        cost_estimate=LONG,
        name="audio_stats",
    )(start, *blocks, video)


def audio_grad(start, blocks, video, stats, video_grads):
    rows, tokens, heads = sizes(blocks, video)
    block = jax.ShapeDtypeStruct(blocks[0].shape, jnp.bfloat16)
    result = pl.pallas_call(
        audio_grad_kernel,
        grid=(heads,),
        in_specs=[pl.BlockSpec(memory_space=pltpu.SMEM)]
        + [head_block(b.shape) for b in blocks]
        + [head_block(video.shape), pl.BlockSpec((1, 2, tokens), lambda h: (h, 0, 0))]
        + [pl.BlockSpec(memory_space=pl.ANY)],
        out_specs=[head_block(b.shape) for b in blocks] + [head_block(video.shape, 1)],
        out_shape=[block] * 4 + [jax.ShapeDtypeStruct(video_grads.shape, jnp.bfloat16)],
        scratch_shapes=[pltpu.VMEM((rows, tokens), jnp.bfloat16)] * 2,
        input_output_aliases={7: 4},
        compiler_params=pltpu.CompilerParams(vmem_limit_bytes=VMEM),
        cost_estimate=LONG,
        name="audio_grad",
    )(start, *blocks, video, stats, video_grads)
    return result[:4], result[4]


def video_all(blocks, video, bias):
    rows, tokens, heads = sizes(blocks, video)
    grads = (video.shape[0], 4) + video.shape[2:]
    block = jax.ShapeDtypeStruct(blocks[0].shape, jnp.bfloat16)
    result = pl.pallas_call(
        video_kernel,
        grid=(heads,),
        in_specs=[head_block(b.shape) for b in blocks]
        + [head_block(video.shape), pl.BlockSpec((tokens, DH), lambda h: (0, 0))],
        out_specs=[head_block(b.shape) for b in blocks] + [head_block(video.shape)],
        out_shape=[block] * 4 + [jax.ShapeDtypeStruct(grads, jnp.bfloat16)],
        scratch_shapes=[pltpu.VMEM((tokens, rows), jnp.bfloat16)] * 2,
        compiler_params=pltpu.CompilerParams(vmem_limit_bytes=VMEM),
        cost_estimate=LONG,
        name="video_all",
    )(*blocks, video, bias)
    return result[:4], result[4]


def exchange(x, axes):
    return lax.all_to_all(x, axes, split_axis=0, concat_axis=0)


def after(x, *others):
    return lax.optimization_barrier((x,) + others)[0]


def video_in(arrays, *others):
    rows, columns = arrays[0].shape
    stack = jnp.stack(arrays).reshape(len(arrays), rows, 8, columns // 8)
    return exchange(after(jnp.transpose(stack, (2, 0, 1, 3)), *others), HEADS8)


def video_out(stack):
    back = jnp.transpose(exchange(stack, HEADS8), (1, 2, 0, 3))
    return back.reshape(back.shape[0], back.shape[1], -1)


def plane_in(arrays, *others):
    stack = jnp.stack(arrays)
    half = stack.shape[-1] // 2
    halves = jnp.stack([stack[..., :half], stack[..., half:]])
    sends = jnp.broadcast_to(halves[None], (8,) + halves.shape)
    return exchange(after(sends.reshape((16,) + halves.shape[1:]), *others), PLANE)


def plane_out(x, *others):
    got = exchange(after(x, *others), PLANE)
    got = got.reshape((8, 2) + got.shape[1:]).astype(jnp.float32).sum(axis=0)
    return jnp.concatenate([got[0], got[1]], axis=-1).astype(jnp.bfloat16)


def along_y(x, step):
    return lax.ppermute(x, "y", [(i, (i + step) % 4) for i in range(4)])


def gather_y(x):
    return [x] + [along_y(x, -step) for step in (1, 2, 3)]


def scatter_y(blocks):
    return [blocks[0]] + [along_y(blocks[step], step) for step in (1, 2, 3)]


def add(parts):
    return sum(part.astype(jnp.float32) for part in parts).astype(jnp.bfloat16)


def merge_stats(stats, axis):
    levels, means = stats
    top = jnp.max(levels, axis=axis, keepdims=True)
    weights = jnp.exp(levels - top)
    total = jnp.sum(weights, axis=axis, keepdims=True)
    mean = jnp.sum(weights * means, axis=axis, keepdims=True) / total
    return jnp.squeeze(top + jnp.log(total), axis), jnp.squeeze(mean, axis)


def per_device(
    video_query,
    video_key,
    video_value,
    video_cotan,
    audio_query,
    audio_key,
    audio_value,
    audio_cotan,
    alignment,
):
    y, zh = lax.axis_index("y"), lax.axis_index("zh")
    frame = y * 4 + zh
    tokens = alignment.shape[0]
    bias = -BIAS_SLOPE * jnp.abs(frame - alignment).astype(jnp.float32)
    start = ((y + jnp.arange(4, dtype=jnp.int32)) % 4) * (tokens // 4)
    turned = lax.dynamic_slice_in_dim(jnp.tile(bias, 2), start[0], tokens)
    key_bias = jnp.broadcast_to((turned * LOG2E)[:, None], (tokens, DH))

    planes = plane_in([audio_query, audio_cotan])
    audio_qg = gather_y(planes)
    video_kv = video_in([video_key, video_value], planes)
    planes = plane_in([audio_key, audio_value], video_kv)
    audio_kv = gather_y(after(planes, audio_qg[1], audio_qg[3]))
    video_qg = video_in([video_query, video_cotan], planes)

    stats = audio_stats(start, audio_qg, video_kv)
    stats = after(jnp.stack([stats[:, 0] + bias, stats[:, 1]]), audio_kv[1], audio_kv[3])
    seen = jnp.stack(merge_stats(jnp.stack(gather_y(stats), axis=1), 0))
    key_bias = after(key_bias, seen)
    seen = jnp.broadcast_to(seen[None], (8,) + seen.shape)
    seen = exchange(after(seen, video_qg), ("zh", "xh"))
    level, inner = merge_stats((seen[:, 0], seen[:, 1]), 0)
    stats = jnp.stack([level - bias, inner], axis=1)

    key_value_blocks, video_grads = video_all(audio_kv, video_qg, key_bias)
    out_query_blocks, video_grads = audio_grad(start, audio_qg, video_kv, stats, video_grads)

    parts = scatter_y(key_value_blocks)
    grads = video_out(after(video_grads, *parts[1:]))
    video_cross_output, video_query_grad, video_key_grad, video_value_grad = grads
    sums = jnp.concatenate([add(parts), add(scatter_y(out_query_blocks))], axis=1)
    sums = plane_out(sums, video_value_grad)
    audio_key_grad, audio_value_grad, audio_cross_output, audio_query_grad = sums
    return (
        video_cross_output,
        audio_cross_output,
        video_query_grad,
        video_key_grad,
        video_value_grad,
        audio_query_grad,
        audio_key_grad,
        audio_value_grad,
    )


def solution(mesh):
    split = Mesh(mesh.devices.reshape(tuple(size for _, size in AXES)), NAMES)
    video = P(NAMES, None)
    audio = P(VID, AUD)
    return jax.shard_map(
        per_device,
        mesh=split,
        in_specs=(video,) * 4 + (audio,) * 4 + (P(),),
        out_specs=(video, audio, video, video, video, audio, audio, audio),
        check_vma=False,
    )
```
